32 devices in a mesh: rep: 8 (over z, y), fsdp: 4 (over x, core).
Axes of the slice: x: 2, y: 2, z: 4, core: 2. Of those that a mesh axis runs over, the one named last changes fastest.
Arguments:
- context: bfloat16 [8, 512, 2560], P('rep', 'fsdp'), may hold values from -6 to 6
- residual: bfloat16 [8, 5120, 512], P('rep', 'fsdp'), may hold values from -6 to 6
- target: bfloat16 [8, 5120, 512], P('rep', 'fsdp'), may hold values from -6 to 6
- norm_gain: float32 [5120], P('fsdp'), may hold values from 0.5 to 1.5
- params: float32 [8, 5120, 2560], P('rep', 'fsdp'), may hold values from -0.3125 to 0.3125
- momentum: bfloat16 [8, 5120, 2560], P('rep', 'fsdp'), may hold values from -0.3125 to 0.3125
- push_weight: float32 [8], P('rep'), may hold values from 0.5 to 2
- mix_num: int32 [8, 3], replicated, may hold values from 1 to 4
Outputs:
- new_params: float32 [8, 5120, 2560], P('rep', 'fsdp')
- new_momentum: bfloat16 [8, 5120, 2560], P('rep', 'fsdp')
- new_push: float32 [8], P('rep')
The draws below stay inside these ranges and needn't reach their ends.
All inputs are finite; a program needn't handle non-finite values.
Results may differ from the reference program's by a relative error of at most 0.0061.
Values may be sent and summed in bfloat16 or wider, within the bound.
No kernel may reach another device: no remote copies, remote signals or barrier semaphores. Data moves between devices by JAX's collectives and lax.ppermute only.
A program may use at most 192 MiB of HBM per device.

```python
import math
import jax
import jax.numpy as jnp
from jax import lax

D = 5120
HD = 2560
TOKENS = 512
STEPS = 2
REPS = 8


def plant(values, rng, least, high):
    index_at = [jax.random.randint(jax.random.fold_in(rng, axis), (), 0, length) for axis, length in enumerate(values.shape)]
    longest = values.shape.index(max(values.shape))
    beside = index_at[:longest] + [(index_at[longest] + 1) % values.shape[longest]] + index_at[longest + 1:]
    return values.at[tuple(index_at)].set(least).at[tuple(beside)].set(high)


def block_scale(rng, shape, split, smallest, top_value):
    def one(axis_at, shards_of):
        steps = jax.random.uniform(jax.random.fold_in(jax.random.fold_in(rng, 6), axis_at), (shards_of,), jnp.float32, smallest / len(split), top_value / len(split))
        return jnp.repeat(jnp.exp(steps), shape[axis_at] // shards_of).reshape((-1,) + (1,) * (len(shape) - axis_at - 1))

    gain = one(*split[0])
    for cut in split[1:]:
        gain = gain * one(*cut)
    return gain


def noise(key, dims, deviation, bound, pieces=(), held_as=jnp.bfloat16):
    result = jax.random.normal(key, dims, jnp.float32) * deviation
    if len(pieces) > 0:
        result = block_scale(key, dims, pieces, -0.22, 0.18) * result
    return jnp.clip(result, min=-bound, max=bound).astype(held_as)


def setup_inputs(seed: int = 0) -> dict:
    key_of = jax.random.split(jax.random.key(seed), 9)
    context = noise(key_of[0], (REPS, TOKENS, HD), 1.0, 6.0, ((0, 8), (1, 4)))
    residual = noise(key_of[1], (REPS, D, TOKENS), 1.0, 6.0, ((0, 8), (1, 4)))
    target = noise(key_of[2], (REPS, D, TOKENS), 1.0, 6.0, ((0, 8), (1, 4)))
    norm_gain = jnp.clip(1.0 + 0.1 * jax.random.normal(key_of[3], (D,), jnp.float32), 0.5, 1.5)
    params = noise(key_of[4], (REPS, D, HD), 0.02, 0.3125, ((0, 8), (1, 4)), jnp.float32)
    momentum = noise(key_of[5], (REPS, D, HD), 0.02, 0.3125, ((0, 8), (1, 4)))
    push_weight = jnp.clip(jnp.exp(math.log(2.0) - 1.3862944 * jax.random.uniform(key_of[6], (REPS,), jnp.float32) ** block_scale(key_of[6], (REPS,), ((0, 8),), -0.2, 0.2)), 0.5, 2.0)
    mix_num = plant(jax.random.randint(key_of[7], (REPS, 3), 1, 5), jax.random.fold_in(key_of[7], 1), 1, 4).astype(jnp.int32)
    return {"context": context, "residual": residual, "target": target, "norm_gain": norm_gain, "params": params, "momentum": momentum, "push_weight": push_weight, "mix_num": mix_num}


epsilon = 1e-05
learn_rate = 0.5
beta_decay = 0.9

def inner_steps(operands):
    context, residual, target, norm_gain, master, moment, push_one = operands
    stream = residual.astype(jnp.float32)
    gain_col = norm_gain[:, None]
    for inner in range(STEPS):
        cast_w = (master / push_one).astype(jnp.bfloat16)
        summed = stream + jnp.dot(cast_w, context.T, preferred_element_type=jnp.float32)
        mean_sq = lax.optimization_barrier(jnp.sum(summed * summed, axis=0)) / D
        inv_rms = lax.rsqrt(mean_sq + epsilon)
        normed = gain_col * summed * inv_rms
        out_grad = (normed - target.astype(jnp.float32)) / TOKENS
        scaled_grad = gain_col * out_grad
        feat_dot = lax.optimization_barrier(jnp.sum(scaled_grad * summed, axis=0)) / D
        stream_grad = (scaled_grad * inv_rms - summed * inv_rms ** 3 * feat_dot).astype(jnp.bfloat16)
        weight_grad = jnp.dot(stream_grad, context, preferred_element_type=jnp.float32)
        moment = (beta_decay * moment.astype(jnp.float32) + weight_grad).astype(jnp.bfloat16)
        master = master - learn_rate * moment.astype(jnp.float32)
    return (master, moment)

def reference(context, residual, target, norm_gain, params, momentum, push_weight, mix_num):
    gains = jnp.broadcast_to(norm_gain, (REPS, D))
    master, moment = lax.map(inner_steps, (context, residual, target, gains, params, momentum, push_weight))
    counts = mix_num.astype(jnp.float32)
    shares = counts / lax.optimization_barrier(jnp.sum(counts, axis=1, keepdims=True))
    keep_share = shares[:, 0]
    lower_share = jnp.roll(shares[:, 2], 1)
    upper_share = jnp.roll(shares[:, 1], -1)

    def mix_cycle(values):
        return keep_share.reshape((-1,) + (1,) * (values.ndim - 1)) * values + lower_share.reshape((-1,) + (1,) * (values.ndim - 1)) * jnp.roll(values, 1, axis=0) + upper_share.reshape((-1,) + (1,) * (values.ndim - 1)) * jnp.roll(values, -1, axis=0)
    new_params = mix_cycle(master)
    new_momentum = mix_cycle(moment.astype(jnp.float32)).astype(jnp.bfloat16)
    new_push = mix_cycle(push_weight)
    return (new_params, new_momentum, new_push)
```

```python
import functools

import jax
import jax.numpy as jnp
from jax import lax
from jax.experimental import pallas as pl
from jax.experimental.pallas import tpu as pltpu
from jax.sharding import PartitionSpec as P

epsilon = 1e-05
learn_rate = 0.5
beta_decay = 0.9

UNIT = 32
VMEM_LIMIT = 56 * 1024 * 1024
F32 = jnp.float32
BF16 = jnp.bfloat16
NT = (((1,), (1,)), ((), ()))

SMEM_SPEC = pl.BlockSpec(memory_space=pltpu.SMEM)


def whole_spec(shape):
    return pl.BlockSpec(shape, lambda i: (0,) * len(shape))


def params_of(limit=VMEM_LIMIT):
    return pltpu.CompilerParams(
        dimension_semantics=("arbitrary",), vmem_limit_bytes=limit
    )


def cost(flops, nbytes):
    return pl.CostEstimate(flops=flops, bytes_accessed=nbytes, transcendentals=0)


def local_tokens(ref, index, count):
    width = ref.shape[1] // count
    blocks = [
        ref[:, pl.ds(pl.multiple_of(lax.bitwise_xor(index, j) * width, width), width)]
        for j in range(count)
    ]
    return jnp.concatenate(blocks, axis=1)


def add_sums(sums_ref, step, total, scaled, target):
    parts = jnp.concatenate(
        [
            jnp.sum(total * total, axis=0, keepdims=True),
            jnp.sum(scaled * scaled, axis=0, keepdims=True),
            jnp.sum(scaled * target, axis=0, keepdims=True),
            jnp.zeros((5, total.shape[1]), F32),
        ],
        axis=0,
    )

    @pl.when(step == 0)
    def _():
        sums_ref[...] = parts

    @pl.when(step > 0)
    def _():
        sums_ref[...] += parts


def token_stats(sum_refs, features):
    count = len(sum_refs)
    tokens = sum_refs[0].shape[1]
    width = tokens // count
    full = sum_refs[0][...]
    for m in range(1, count):
        other = sum_refs[m]
        full = full + jnp.concatenate(
            [other[:, (j ^ m) * width : ((j ^ m) + 1) * width] for j in range(count)],
            axis=1,
        )
    inv = lax.rsqrt(full[0:1] / features + epsilon)
    dot = (inv * full[1:2] - full[2:3]) / (tokens * features)
    return inv, dot


def stream_grad(total, target, gain, inv, dot, tokens):
    scaled = gain * ((gain * total * inv - target) / tokens)
    return (scaled * inv - total * (inv * inv * inv * dot)).astype(BF16)


def forward_kernel(
    count, idx_ref, coef_ref, p_ref, m_ref, c_ref, r_ref, t_ref, g_ref, s_ref, y_ref, q_ref
):
    index = idx_ref[0]
    weights = (p_ref[...] * coef_ref[0]).astype(BF16)
    context = c_ref[...]
    product = lax.dot_general(weights, context, NT, preferred_element_type=F32)
    y_ref[...] = lax.dot_general(m_ref[...], context, NT, preferred_element_type=F32)
    total = local_tokens(r_ref, index, count).astype(F32) + product
    s_ref[...] = total
    target = local_tokens(t_ref, index, count).astype(F32)
    add_sums(q_ref, pl.program_id(0), total, g_ref[...] * total, target)


def forward(index, coef, params, moment, context, residual, target, gain, count):
    rows, width = params.shape
    tokens = context.shape[0]
    block = min(128, rows)
    row = lambda n: pl.BlockSpec((block, n), lambda i: (i, 0))
    return pl.pallas_call(
        functools.partial(forward_kernel, count),
        grid=(rows // block,),
        in_specs=[
            SMEM_SPEC,
            SMEM_SPEC,
            row(width),
            row(width),
            whole_spec((tokens, width)),
            row(tokens),
            row(tokens),
            row(1),
        ],
        out_specs=[row(tokens), row(tokens), whole_spec((8, tokens))],
        out_shape=[
            jax.ShapeDtypeStruct((rows, tokens), F32),
            jax.ShapeDtypeStruct((rows, tokens), F32),
            jax.ShapeDtypeStruct((8, tokens), F32),
        ],
        compiler_params=params_of(),
        cost_estimate=cost(4 * rows * width * tokens, rows * width * 6),
    )(index, coef, params, moment, context, residual, target, gain)


def second_kernel(count, features, idx_ref, coef_ref, s_ref, t_ref, g_ref, y_ref, gram_ref, *rest):
    sum_refs, (grad_ref, s2_ref, q_ref, high_ref, low_ref) = rest[:count], rest[count:]
    index = idx_ref[0]
    step = pl.program_id(0)

    @pl.when(step == 0)
    def _():
        gram = gram_ref[...]
        high = gram.astype(BF16)
        high_ref[...] = high
        low_ref[...] = (gram - high.astype(F32)).astype(BF16)

    inv, dot = token_stats(sum_refs, features)
    total = s_ref[...]
    target = local_tokens(t_ref, index, count).astype(F32)
    gain = g_ref[...]
    grad = stream_grad(total, target, gain, inv, dot, total.shape[1])
    grad_ref[...] = grad
    moved = jnp.dot(grad, high_ref[...], preferred_element_type=F32)
    moved += jnp.dot(grad, low_ref[...], preferred_element_type=F32)
    total = total - coef_ref[1] * (beta_decay * y_ref[...] + moved)
    s2_ref[...] = total
    add_sums(q_ref, step, total, gain * total, target)


def second(index, coef, total, target, gain, moment_product, gram, sums, features):
    rows, tokens = total.shape
    count = len(sums)
    block = min(256, rows) if rows % 256 == 0 else min(64, rows)
    row = lambda n: pl.BlockSpec((block, n), lambda i: (i, 0))
    return pl.pallas_call(
        functools.partial(second_kernel, count, features),
        grid=(rows // block,),
        in_specs=[
            SMEM_SPEC,
            SMEM_SPEC,
            row(tokens),
            row(tokens),
            row(1),
            row(tokens),
            pl.BlockSpec((tokens, tokens), lambda i: (0, 0), pipeline_mode=pl.Buffered(1)),
        ]
        + [whole_spec((8, tokens))] * count,
        out_specs=[row(tokens), row(tokens), whole_spec((8, tokens))],
        out_shape=[
            jax.ShapeDtypeStruct((rows, tokens), BF16),
            jax.ShapeDtypeStruct((rows, tokens), F32),
            jax.ShapeDtypeStruct((8, tokens), F32),
        ],
        scratch_shapes=[pltpu.VMEM((tokens, tokens), BF16)] * 2,
        compiler_params=params_of(),
        cost_estimate=cost(4 * rows * tokens * tokens, rows * tokens * 16),
    )(index, coef, total, target, gain, moment_product, gram, *sums)


def update_kernel(count, features, idx_ref, p_ref, m_ref, grad_ref, s_ref, t_ref, g_ref, c_ref, *rest):
    sum_refs, (out_ref, master_ref) = rest[:count], rest[count:]
    inv, dot = token_stats(sum_refs, features)
    target = local_tokens(t_ref, idx_ref[0], count).astype(F32)
    grad2 = stream_grad(s_ref[...], target, g_ref[...], inv, dot, s_ref.shape[1])
    rows = grad2.shape[0]
    both = jnp.dot(
        jnp.concatenate([grad_ref[...], grad2], axis=0), c_ref[...], preferred_element_type=F32
    )
    moment = (beta_decay * m_ref[...].astype(F32) + both[:rows]).astype(BF16).astype(F32)
    master = p_ref[...] - learn_rate * moment
    moment = (beta_decay * moment + both[rows:]).astype(BF16)
    master = master - learn_rate * moment.astype(F32)
    out_ref[0] = master.astype(BF16)
    out_ref[1] = moment
    master_ref[...] = master


def update(start, units, index, params, moment, grad, total, target, gain, context, sums, features):
    width = params.shape[1]
    tokens = total.shape[1]
    count = len(sums)
    rows = units * UNIT
    row = lambda n: pl.BlockSpec((UNIT, n), lambda i: (start + i, 0))
    return pl.pallas_call(
        functools.partial(update_kernel, count, features),
        grid=(units,),
        in_specs=[
            SMEM_SPEC,
            row(width),
            row(width),
            row(tokens),
            row(tokens),
            row(tokens),
            row(1),
            whole_spec((tokens, width)),
        ]
        + [whole_spec((8, tokens))] * count,
        out_specs=[
            pl.BlockSpec((2, UNIT, width), lambda i: (0, i, 0)),
            pl.BlockSpec((UNIT, width), lambda i: (i, 0)),
        ],
        out_shape=[
            jax.ShapeDtypeStruct((2, rows, width), BF16),
            jax.ShapeDtypeStruct((rows, width), F32),
        ],
        compiler_params=params_of(),
        cost_estimate=cost(4 * rows * width * tokens, rows * width * 14),
    )(index, params, moment, grad, total, target, gain, context, *sums)


def pair_kernel(coef_ref, master_ref, state_ref, other_ref, out_ref):
    mine, theirs = coef_ref[2], coef_ref[3]
    out_ref[0] = (mine * master_ref[...] + theirs * other_ref[0].astype(F32)).astype(BF16)
    out_ref[1] = (mine * state_ref[0].astype(F32) + theirs * other_ref[1].astype(F32)).astype(BF16)


def pair_sum(coef, master, state, other):
    _, rows, width = state.shape
    block = UNIT
    return pl.pallas_call(
        pair_kernel,
        grid=(rows // block,),
        in_specs=[
            SMEM_SPEC,
            pl.BlockSpec((block, width), lambda i: (i, 0)),
            pl.BlockSpec((1, block, width), lambda i: (1, i, 0)),
            pl.BlockSpec((2, block, width), lambda i: (0, i, 0)),
        ],
        out_specs=pl.BlockSpec((2, block, width), lambda i: (0, i, 0)),
        out_shape=jax.ShapeDtypeStruct((2, rows, width), BF16),
        compiler_params=params_of(),
        cost_estimate=cost(6 * rows * width, rows * width * 14),
    )(coef, master, state, other)


def final_kernel(coef_ref, master_ref, state_ref, sum_ref, *rest):
    p_ref, m_ref = rest[-2:]
    keep = coef_ref[4]
    p_ref[...] = keep * master_ref[...] + sum_ref[0].astype(F32)
    m_ref[...] = (keep * state_ref[0].astype(F32) + sum_ref[1].astype(F32)).astype(BF16)


def final(start, total_rows, coef, master, state, arrived, held):
    _, rows, width = state.shape
    block = UNIT
    out = pl.BlockSpec((block, width), lambda i: (start + i, 0))
    held = held or ()
    return pl.pallas_call(
        final_kernel,
        grid=(rows // block,),
        in_specs=[
            SMEM_SPEC,
            pl.BlockSpec((block, width), lambda i: (i, 0)),
            pl.BlockSpec((1, block, width), lambda i: (1, i, 0)),
            pl.BlockSpec((2, block, width), lambda i: (0, i, 0)),
        ]
        + [pl.BlockSpec(memory_space=pl.ANY)] * len(held),
        out_specs=[out, out],
        out_shape=[
            jax.ShapeDtypeStruct((total_rows, width), F32),
            jax.ShapeDtypeStruct((total_rows, width), BF16),
        ],
        input_output_aliases={4: 0, 5: 1} if held else {},
        compiler_params=params_of(),
        cost_estimate=cost(4 * rows * width, rows * width * 16),
    )(coef, master, state, arrived, *held)


def with_partner(value, distance, count):
    return lax.ppermute(value, "fsdp", [(i, i ^ distance) for i in range(count)])


def gather_tokens(block, count):
    pieces = {0: block}
    distance = count // 2
    while distance:
        for j in list(pieces):
            pieces[j | distance] = with_partner(pieces[j], distance, count)
        distance //= 2
    return jnp.concatenate([pieces[j] for j in range(count)], axis=0)


def all_sums(sums, count):
    return [sums] + [with_partner(sums, m, count) for m in range(1, count)]


def local(context, residual, target, norm_gain, params, momentum, push_weight, mix_num):
    count = lax.axis_size("fsdp")
    replicas = lax.axis_size("rep")
    replica = lax.axis_index("rep")
    index = lax.axis_index("fsdp").astype(jnp.int32)[None]
    residual, target, params, momentum = residual[0], target[0], params[0], momentum[0]
    rows, width = params.shape
    features = rows * count

    shares = mix_num.astype(F32)
    shares = shares / jnp.sum(shares, axis=1, keepdims=True)
    even = replica % 2 == 0
    away = jnp.where(even, (replica + 2) % replicas, (replica - 2) % replicas)
    mine = jnp.where(even, shares[replica, 2], shares[replica, 1])
    theirs = jnp.where(even, shares[away, 1], shares[away, 2])
    keep = shares[replica, 0]
    push = push_weight[0]
    zero = jnp.zeros((), F32)
    coef = jnp.stack([1.0 / push, learn_rate / push, mine, theirs, keep, zero, zero, zero])

    along_z = [(r, (r - 2) % replicas if r % 2 == 0 else (r + 2) % replicas) for r in range(replicas)]
    along_y = [(r, r ^ 1) for r in range(replicas)]

    tokens_all = gather_tokens(context[0], count)
    gain = norm_gain[:, None]
    total, moment_product, sums = forward(
        index, coef, params, momentum, tokens_all, residual, target, gain, count
    )
    sums = all_sums(sums, count)
    gram = lax.dot_general(tokens_all, tokens_all, NT, preferred_element_type=F32)
    grad, total, sums = second(
        index, coef, total, target, gain, moment_product, gram, sums, features
    )
    sums = all_sums(sums, count)

    units = 1
    starts = list(range(0, rows // UNIT, units))
    held = None
    chunks = []
    for start in starts:
        state, master = update(
            start, units, index, params, momentum, grad, total, target, gain, tokens_all, sums, features
        )
        chunks.append((state, master, lax.ppermute(state, "rep", along_z)))
    for at, (state, master, other) in enumerate(chunks):
        both = pair_sum(coef, master, state, other)
        chunks[at] = (state, master, lax.ppermute(both, "rep", along_y))
    for start, (state, master, arrived) in zip(starts, chunks):
        held = final(start, rows, coef, master, state, arrived, held)

    push_row = jnp.broadcast_to(push, (8, 128))
    push_other = lax.ppermute(push_row, "rep", along_z)
    push_sum = lax.ppermute(mine * push_row + theirs * push_other, "rep", along_y)
    new_push = keep * push + push_sum[0, 0]
    return (held[0][None], held[1][None], new_push[None])


def solution(mesh):
    return jax.shard_map(
        local,
        mesh=mesh,
        in_specs=(
            P("rep", "fsdp", None),
            P("rep", "fsdp", None),
            P("rep", "fsdp", None),
            P("fsdp"),
            P("rep", "fsdp", None),
            P("rep", "fsdp", None),
            P("rep"),
            P(),
        ),
        out_specs=(P("rep", "fsdp", None), P("rep", "fsdp", None), P("rep")),
        check_vma=False,
    )
```

```python
import functools

import jax
import jax.numpy as jnp
from jax import lax
from jax.experimental import pallas as pl
from jax.experimental.pallas import tpu as pltpu
from jax.sharding import PartitionSpec as P

epsilon = 1e-05
learn_rate = 0.5
beta_decay = 0.9

UNIT = 32
CHUNK = 64
Z_AHEAD = 3
Y_AHEAD = 2
MIB = 1024 * 1024
FORWARD_ROWS = 256
FORWARD_MIB = SECOND_MIB = STEP_MIB = PAIR_MIB = 24
F32 = jnp.float32
BF16 = jnp.bfloat16
NT = (((1,), (1,)), ((), ()))

SMEM_SPEC = pl.BlockSpec(memory_space=pltpu.SMEM)


def whole_spec(shape):
    return pl.BlockSpec(shape, lambda i: (0,) * len(shape))


def params_of(limit):
    return pltpu.CompilerParams(
        dimension_semantics=("arbitrary",), vmem_limit_bytes=limit
    )


def cost(flops, nbytes):
    return pl.CostEstimate(flops=flops, bytes_accessed=nbytes, transcendentals=0)


def shares_of(mix_ref):
    replicas = mix_ref.shape[0] // 3
    replica = lax.axis_index("rep")
    odd = lax.rem(replica, 2)
    away = lax.rem(replica + jnp.where(odd == 1, replicas - 2, 2), replicas)

    def share(at, column):
        row = [mix_ref[3 * at + k].astype(F32) for k in range(3)]
        return mix_ref[3 * at + column].astype(F32) / (row[0] + row[1] + row[2])

    return share(replica, 0), share(replica, 2 - odd), share(away, 1 + odd)


def neighbour_shares(mix_ref):
    replicas = mix_ref.shape[0] // 3
    replica = lax.axis_index("rep")

    def share(at, column):
        row = [mix_ref[3 * at + k].astype(F32) for k in range(3)]
        return row[column] / (row[0] + row[1] + row[2])

    lower = lax.rem(replica + replicas - 1, replicas)
    upper = lax.rem(replica + 1, replicas)
    return share(replica, 0), share(lower, 2), share(upper, 1)


def local_tokens(ref, index, count):
    width = ref.shape[1] // count
    blocks = [
        ref[:, pl.ds(pl.multiple_of(lax.bitwise_xor(index, j) * width, width), width)]
        for j in range(count)
    ]
    return jnp.concatenate(blocks, axis=1)


def add_sums(sums_ref, step, total, scaled, target):
    parts = jnp.concatenate(
        [
            jnp.sum(total * total, axis=0, keepdims=True),
            jnp.sum(scaled * scaled, axis=0, keepdims=True),
            jnp.sum(scaled * target, axis=0, keepdims=True),
            jnp.zeros((5, total.shape[1]), F32),
        ],
        axis=0,
    )

    @pl.when(step == 0)
    def _():
        sums_ref[...] = parts

    @pl.when(step > 0)
    def _():
        sums_ref[...] += parts


def token_stats(sum_refs, features):
    count = len(sum_refs)
    tokens = sum_refs[0].shape[1]
    width = tokens // count
    full = sum_refs[0][...]
    for m in range(1, count):
        other = sum_refs[m]
        full = full + jnp.concatenate(
            [other[:, (j ^ m) * width : ((j ^ m) + 1) * width] for j in range(count)],
            axis=1,
        )
    inv = lax.rsqrt(full[0:1] / features + epsilon)
    dot = (inv * full[1:2] - full[2:3]) / (tokens * features)
    return inv, dot


def stream_grad(total, target, gain, inv, dot, tokens):
    scaled = gain * ((gain * total * inv - target) / tokens)
    return (scaled * inv - total * (inv * inv * inv * dot)).astype(BF16)


def transpose_pieces(piece_refs, out_ref):
    width = piece_refs[0].shape[0]
    for j, piece in enumerate(piece_refs):
        out_ref[:, j * width : (j + 1) * width] = piece[...].T


def forward_kernel(count, mix_ref, push_ref, low_ref, high_ref, p_ref, m_ref, r_ref, t_ref, g_ref, *rest):
    pieces, (s_ref, y_ref, q_ref, c_ref, push_out, ct_ref) = rest[:count], rest[count:]
    index = lax.axis_index("fsdp")
    step = pl.program_id(0)

    @pl.when(step == 0)
    def _():
        transpose_pieces(pieces, ct_ref)
        width = pieces[0].shape[0]
        for j, piece in enumerate(pieces):
            c_ref[j * width : (j + 1) * width, :] = piece[...]
        keep, lower, upper = neighbour_shares(mix_ref)
        push_out[...] = keep * push_ref[0] + lower * low_ref[...] + upper * high_ref[...]

    rows = p_ref.shape[0]
    weights = (p_ref[...] * (1.0 / push_ref[0])).astype(BF16)
    both = jnp.concatenate([weights, m_ref[...]], axis=0)
    product = jnp.dot(both, ct_ref[...], preferred_element_type=F32)
    y_ref[...] = product[rows:]
    total = local_tokens(r_ref, index, count).astype(F32) + product[:rows]
    s_ref[...] = total
    target = local_tokens(t_ref, index, count).astype(F32)
    add_sums(q_ref, step, total, g_ref[...] * total, target)


def forward(mix, push, lower, upper, params, moment, residual, target, gain, pieces):
    rows, width = params.shape
    piece = pieces[0].shape[0]
    count = len(pieces)
    tokens = piece * count
    block = FORWARD_ROWS if rows % FORWARD_ROWS == 0 else 64
    row = lambda n: pl.BlockSpec((block, n), lambda i: (i, 0))
    return pl.pallas_call(
        functools.partial(forward_kernel, count),
        grid=(rows // block,),
        in_specs=[
            SMEM_SPEC,
            SMEM_SPEC,
            whole_spec((8, 128)),
            whole_spec((8, 128)),
            row(width),
            row(width),
            row(tokens),
            row(tokens),
            row(1),
        ]
        + [whole_spec((piece, width))] * count,
        out_specs=[
            row(tokens),
            row(tokens),
            whole_spec((8, tokens)),
            whole_spec((tokens, width)),
            whole_spec((8, 128)),
        ],
        out_shape=[
            jax.ShapeDtypeStruct((rows, tokens), F32),
            jax.ShapeDtypeStruct((rows, tokens), F32),
            jax.ShapeDtypeStruct((8, tokens), F32),
            jax.ShapeDtypeStruct((tokens, width), BF16),
            jax.ShapeDtypeStruct((8, 128), F32),
        ],
        scratch_shapes=[pltpu.VMEM((width, tokens), BF16)],
        compiler_params=params_of(FORWARD_MIB * MIB if tokens <= 512 else 58 * MIB),
        cost_estimate=cost(4 * rows * width * tokens, rows * width * 6),
    )(mix, push, lower, upper, params, moment, residual, target, gain, *pieces)


def second_kernel(count, features, push_ref, s_ref, t_ref, g_ref, y_ref, gram_ref, *rest):
    sum_refs, (grad_ref, s2_ref, q_ref, high_ref, low_ref) = rest[:count], rest[count:]
    index = lax.axis_index("fsdp")
    step = pl.program_id(0)

    @pl.when(step == 0)
    def _():
        gram = gram_ref[...]
        high = gram.astype(BF16)
        high_ref[...] = high
        low_ref[...] = (gram - high.astype(F32)).astype(BF16)

    inv, dot = token_stats(sum_refs, features)
    total = s_ref[...]
    target = local_tokens(t_ref, index, count).astype(F32)
    gain = g_ref[...]
    grad = stream_grad(total, target, gain, inv, dot, total.shape[1])
    grad_ref[...] = grad
    moved = jnp.dot(grad, high_ref[...], preferred_element_type=F32)
    moved += jnp.dot(grad, low_ref[...], preferred_element_type=F32)
    total = total - (learn_rate / push_ref[0]) * (beta_decay * y_ref[...] + moved)
    s2_ref[...] = total
    add_sums(q_ref, step, total, gain * total, target)


def second(push, total, target, gain, moment_product, gram, sums, features):
    rows, tokens = total.shape
    count = len(sums)
    block = min(256, rows) if rows % 256 == 0 else min(64, rows)
    row = lambda n: pl.BlockSpec((block, n), lambda i: (i, 0))
    return pl.pallas_call(
        functools.partial(second_kernel, count, features),
        grid=(rows // block,),
        in_specs=[
            SMEM_SPEC,
            row(tokens),
            row(tokens),
            row(1),
            row(tokens),
            pl.BlockSpec((tokens, tokens), lambda i: (0, 0), pipeline_mode=pl.Buffered(1)),
        ]
        + [whole_spec((8, tokens))] * count,
        out_specs=[row(tokens), row(tokens), whole_spec((8, tokens))],
        out_shape=[
            jax.ShapeDtypeStruct((rows, tokens), BF16),
            jax.ShapeDtypeStruct((rows, tokens), F32),
            jax.ShapeDtypeStruct((8, tokens), F32),
        ],
        scratch_shapes=[pltpu.VMEM((tokens, tokens), BF16)] * 2,
        compiler_params=params_of(SECOND_MIB * MIB if tokens <= 512 else 56 * MIB),
        cost_estimate=cost(4 * rows * tokens * tokens, rows * tokens * 16),
    )(push, total, target, gain, moment_product, gram, *sums)


def step_kernel(count, features, has_update, has_final, waits, *refs):
    refs = list(refs)
    take = lambda n: [refs.pop(0) for _ in range(n)]
    (mix_ref,) = take(1)
    if has_update:
        p_in, m_in, grad_ref, s_ref, t_ref, g_ref, c_ref = take(7)
        sum_refs = take(count)
    if has_final:
        master_in, state_in, arrived_ref = take(3)
    take(waits)
    if has_update:
        state_ref, master_ref = take(2)
        inv, dot = token_stats(sum_refs, features)
        target = local_tokens(t_ref, lax.axis_index("fsdp"), count).astype(F32)
        grad2 = stream_grad(s_ref[...], target, g_ref[...], inv, dot, s_ref.shape[1])
        rows = grad2.shape[0]
        both = jnp.dot(
            jnp.concatenate([grad_ref[...], grad2], axis=0),
            c_ref[...],
            preferred_element_type=F32,
        )
        moment = (beta_decay * m_in[...].astype(F32) + both[:rows]).astype(BF16).astype(F32)
        master = p_in[...] - learn_rate * moment
        moment = (beta_decay * moment + both[rows:]).astype(BF16)
        master = master - learn_rate * moment.astype(F32)
        state_ref[0] = master.astype(BF16)
        state_ref[1] = moment
        master_ref[...] = master
    if has_final:
        p_out, m_out = take(2)
        keep, _, _ = shares_of(mix_ref)
        p_out[...] = keep * master_in[...] + arrived_ref[0].astype(F32)
        m_out[...] = (keep * state_in[0].astype(F32) + arrived_ref[1].astype(F32)).astype(BF16)


def step_call(mix, rows, update, done, held, after, features):
    units = rows // UNIT
    operands, specs, out_specs, out_shape = [mix], [SMEM_SPEC], [], []
    count = 0
    flops = nbytes = 0
    if update:
        start, arrays, sums = update
        params, moment, grad, total, target, gain, context = arrays
        width, tokens, count = params.shape[1], total.shape[1], len(sums)
        first = start // UNIT
        row = lambda n: pl.BlockSpec((UNIT, n), lambda i: (first + i, 0))
        operands += [*arrays, *sums]
        specs += [row(width), row(width), row(tokens), row(tokens), row(tokens), row(1)]
        specs += [whole_spec((tokens, width))] + [whole_spec((8, tokens))] * count
        flops += 4 * rows * width * tokens
        nbytes += rows * width * 14
    if done:
        begin, all_rows, master, state, arrived = done
        width = master.shape[1]
        operands += [master, state, arrived]
        specs += [
            pl.BlockSpec((UNIT, width), lambda i: (i, 0)),
            pl.BlockSpec((1, UNIT, width), lambda i: (1, i, 0)),
            pl.BlockSpec((2, UNIT, width), lambda i: (0, i, 0)),
        ]
        nbytes += rows * width * 16
    waits = [*(held if done and held else ()), *after]
    alias = {}
    if done and held:
        alias = {len(operands): 2 if update else 0, len(operands) + 1: 3 if update else 1}
    operands += waits
    specs += [pl.BlockSpec(memory_space=pl.ANY)] * len(waits)
    if update:
        out_specs += [
            pl.BlockSpec((2, UNIT, width), lambda i: (0, i, 0)),
            pl.BlockSpec((UNIT, width), lambda i: (i, 0)),
        ]
        out_shape += [
            jax.ShapeDtypeStruct((2, rows, width), BF16),
            jax.ShapeDtypeStruct((rows, width), F32),
        ]
    if done:
        at = begin // UNIT
        out_specs += [pl.BlockSpec((UNIT, width), lambda i: (at + i, 0))] * 2
        out_shape += [
            jax.ShapeDtypeStruct((all_rows, width), F32),
            jax.ShapeDtypeStruct((all_rows, width), BF16),
        ]
    out = pl.pallas_call(
        functools.partial(
            step_kernel, count, features, bool(update), bool(done), len(waits)
        ),
        grid=(units,),
        in_specs=specs,
        out_specs=out_specs,
        out_shape=out_shape,
        input_output_aliases=alias,
        compiler_params=params_of(STEP_MIB * MIB),
        cost_estimate=cost(flops, nbytes),
    )(*operands)
    made = tuple(out[:2]) if update else None
    return made, tuple(out[-2:]) if done else held


def pair_kernel(mix_ref, master_ref, state_ref, other_ref, *rest):
    out_ref = rest[-1]
    _, mine, theirs = shares_of(mix_ref)
    out_ref[0] = (mine * master_ref[...] + theirs * other_ref[0].astype(F32)).astype(BF16)
    out_ref[1] = (mine * state_ref[0].astype(F32) + theirs * other_ref[1].astype(F32)).astype(BF16)


def pair_sum(mix, master, state, other, after):
    _, rows, width = state.shape
    return pl.pallas_call(
        pair_kernel,
        grid=(rows // UNIT,),
        in_specs=[
            SMEM_SPEC,
            pl.BlockSpec((UNIT, width), lambda i: (i, 0)),
            pl.BlockSpec((1, UNIT, width), lambda i: (1, i, 0)),
            pl.BlockSpec((2, UNIT, width), lambda i: (0, i, 0)),
        ]
        + [pl.BlockSpec(memory_space=pl.ANY)] * len(after),
        out_specs=pl.BlockSpec((2, UNIT, width), lambda i: (0, i, 0)),
        out_shape=jax.ShapeDtypeStruct((2, rows, width), BF16),
        compiler_params=params_of(PAIR_MIB * MIB),
        cost_estimate=cost(6 * rows * width, rows * width * 14),
    )(mix, master, state, other, *after)


def with_partner(value, distance, count):
    return lax.ppermute(value, "fsdp", [(i, i ^ distance) for i in range(count)])


def gather_low(block, count):
    pieces = {0: block}
    distance = count // 4
    while distance:
        for j in list(pieces):
            pieces[j | distance] = with_partner(pieces[j], distance, count)
        distance //= 2
    return [pieces[j] for j in sorted(pieces)]


def all_sums(sums, count):
    return [sums] + [with_partner(sums, m, count) for m in range(1, count)]


def local(context, residual, target, norm_gain, params, momentum, push_weight, mix_num):
    count = lax.axis_size("fsdp")
    replicas = lax.axis_size("rep")
    residual, target, params, momentum = residual[0], target[0], params[0], momentum[0]
    rows, width = params.shape
    features = rows * count

    along_z = [(r, (r - 2) % replicas if r % 2 == 0 else (r + 2) % replicas) for r in range(replicas)]
    along_y = [(r, r ^ 1) for r in range(replicas)]
    over_z = lambda value: lax.ppermute(value, "rep", along_z)
    over_y = lambda value: lax.ppermute(value, "rep", along_y)

    far = with_partner(context[0], count // 2, count)
    near_pieces = gather_low(context[0], count)
    push_row = jnp.broadcast_to(push_weight, (8, 128))
    push_lower = lax.ppermute(push_row, "rep", [(r, (r + 1) % replicas) for r in range(replicas)])
    push_upper = lax.ppermute(push_row, "rep", [(r, (r - 1) % replicas) for r in range(replicas)])
    gain = norm_gain[:, None]
    mix = mix_num.reshape(-1)
    far, gain, push_lower, push_upper, mix, *near_pieces = lax.optimization_barrier(
        (far, gain, push_lower, push_upper, mix, *near_pieces)
    )
    pieces = near_pieces + gather_low(far, count)
    total, moment_product, sums, tokens_all, new_push = forward(
        mix,
        push_weight,
        push_lower,
        push_upper,
        params,
        momentum,
        residual,
        target,
        gain,
        pieces,
    )
    sums = all_sums(sums, count)
    gram = lax.dot_general(tokens_all, tokens_all, NT, preferred_element_type=F32)
    grad, total, sums = second(
        push_weight, total, target, gain, moment_product, gram, sums, features
    )
    sums = all_sums(sums, count)

    arrays = (params, momentum, grad, total, target, gain, tokens_all)
    chunk = CHUNK if rows % CHUNK == 0 else UNIT
    chunks = rows // chunk
    made, crossing, arriving = {}, {}, {}
    held = None
    last = ()
    for c in range(-Z_AHEAD, chunks + Y_AHEAD):
        if 0 <= c < chunks:
            state, master = made[c]
            both = pair_sum(mix, master, state, crossing.pop(c), last)
            arriving[c] = over_y(both)
            last = (both,)
        ahead, behind = c + Z_AHEAD, c - Y_AHEAD
        update = (ahead * chunk, arrays, sums) if ahead < chunks else None
        done = None
        if behind >= 0:
            state, master = made.pop(behind)
            done = (behind * chunk, rows, master, state, arriving.pop(behind))
        if update or done:
            out, held = step_call(mix, chunk, update, done, held, last, features)
            if out:
                made[ahead] = out
                crossing[ahead] = over_z(out[0])
                last = (out[0],)
    return (held[0][None], held[1][None], new_push[0, 0:1])


def solution(mesh):
    return jax.shard_map(
        local,
        mesh=mesh,
        in_specs=(
            P("rep", "fsdp", None),
            P("rep", "fsdp", None),
            P("rep", "fsdp", None),
            P("fsdp"),
            P("rep", "fsdp", None),
            P("rep", "fsdp", None),
            P("rep"),
            P(),
        ),
        out_specs=(P("rep", "fsdp", None), P("rep", "fsdp", None), P("rep")),
        check_vma=False,
    )
```

```python
import functools

import jax
import jax.numpy as jnp
from jax import lax
from jax.experimental import pallas as pl
from jax.experimental.pallas import tpu as pltpu
from jax.sharding import PartitionSpec as P

epsilon = 1e-05
learn_rate = 0.5
beta_decay = 0.9

UNIT = 32
CHUNKS = ((64, 1),)
Z_AHEAD = 2
Y_AHEAD = 1
MIB = 1024 * 1024
FORWARD_ROWS = 256
FORWARD_MIB = SECOND_MIB = STEP_MIB = PAIR_MIB = 24
F32 = jnp.float32
BF16 = jnp.bfloat16
NT = (((1,), (1,)), ((), ()))

SMEM_SPEC = pl.BlockSpec(memory_space=pltpu.SMEM)


def whole_spec(shape):
    return pl.BlockSpec(shape, lambda i: (0,) * len(shape))


def params_of(limit):
    return pltpu.CompilerParams(
        dimension_semantics=("arbitrary",), vmem_limit_bytes=limit
    )


def cost(flops, nbytes):
    return pl.CostEstimate(flops=flops, bytes_accessed=nbytes, transcendentals=0)


def shares_of(mix_ref):
    replicas = mix_ref.shape[0] // 3
    replica = lax.axis_index("rep")
    odd = lax.rem(replica, 2)
    away = lax.rem(replica + jnp.where(odd == 1, replicas - 2, 2), replicas)

    def share(at, column):
        row = [mix_ref[3 * at + k].astype(F32) for k in range(3)]
        return mix_ref[3 * at + column].astype(F32) / (row[0] + row[1] + row[2])

    return share(replica, 0), share(replica, 2 - odd), share(away, 1 + odd)


def neighbour_shares(mix_ref):
    replicas = mix_ref.shape[0] // 3
    replica = lax.axis_index("rep")

    def share(at, column):
        row = [mix_ref[3 * at + k].astype(F32) for k in range(3)]
        return row[column] / (row[0] + row[1] + row[2])

    lower = lax.rem(replica + replicas - 1, replicas)
    upper = lax.rem(replica + 1, replicas)
    return share(replica, 0), share(lower, 2), share(upper, 1)


def local_tokens(ref, index, count):
    width = ref.shape[1] // count
    blocks = [
        ref[:, pl.ds(pl.multiple_of(lax.bitwise_xor(index, j) * width, width), width)]
        for j in range(count)
    ]
    return jnp.concatenate(blocks, axis=1)


def add_sums(sums_ref, step, total, scaled, target):
    parts = jnp.concatenate(
        [
            jnp.sum(total * total, axis=0, keepdims=True),
            jnp.sum(scaled * scaled, axis=0, keepdims=True),
            jnp.sum(scaled * target, axis=0, keepdims=True),
            jnp.zeros((5, total.shape[1]), F32),
        ],
        axis=0,
    )

    @pl.when(step == 0)
    def _():
        sums_ref[...] = parts

    @pl.when(step > 0)
    def _():
        sums_ref[...] += parts


def token_stats(sum_refs, features):
    count = len(sum_refs)
    tokens = sum_refs[0].shape[1]
    width = tokens // count
    full = sum_refs[0][...]
    for m in range(1, count):
        other = sum_refs[m]
        full = full + jnp.concatenate(
            [other[:, (j ^ m) * width : ((j ^ m) + 1) * width] for j in range(count)],
            axis=1,
        )
    inv = lax.rsqrt(full[0:1] / features + epsilon)
    dot = (inv * full[1:2] - full[2:3]) / (tokens * features)
    return inv, dot


def stream_grad(total, target, gain, inv, dot, tokens):
    scaled = gain * ((gain * total * inv - target) / tokens)
    return (scaled * inv - total * (inv * inv * inv * dot)).astype(BF16)


def transpose_pieces(piece_refs, out_ref):
    width = piece_refs[0].shape[0]
    for j, piece in enumerate(piece_refs):
        out_ref[:, j * width : (j + 1) * width] = piece[...].T


def near_kernel(count, *refs):
    transpose_pieces(refs[:count], refs[-1])


def near_turned(pieces, mix, beside):
    piece, width = pieces[0].shape
    tokens = piece * len(pieces)
    return pl.pallas_call(
        functools.partial(near_kernel, len(pieces)),
        grid=(1,),
        in_specs=[whole_spec((piece, width))] * len(pieces)
        + [SMEM_SPEC]
        + [pl.BlockSpec(memory_space=pl.ANY)] * len(beside),
        out_specs=whole_spec((width, tokens)),
        out_shape=jax.ShapeDtypeStruct((width, tokens), BF16),
        compiler_params=params_of(FORWARD_MIB * MIB),
        cost_estimate=cost(2 * tokens * width, 4 * tokens * width),
    )(*pieces, mix, *beside)


def forward_kernel(
    count, mix_ref, push_ref, low_ref, high_ref, p_ref, m_ref, r_ref, t_ref, g_ref, near_ref, *rest
):
    pieces, (s_ref, y_ref, q_ref, c_ref, push_out, ct_ref) = rest[:count], rest[count:]
    index = lax.axis_index("fsdp")
    step = pl.program_id(0)

    @pl.when(step == 0)
    def _():
        half = near_ref.shape[1]
        ct_ref[:, :half] = near_ref[...]
        transpose_pieces(pieces[count // 2 :], ct_ref.at[:, half:])
        width = pieces[0].shape[0]
        for j, piece in enumerate(pieces):
            c_ref[j * width : (j + 1) * width, :] = piece[...]
        keep, lower, upper = neighbour_shares(mix_ref)
        push_out[...] = keep * push_ref[0] + lower * low_ref[...] + upper * high_ref[...]

    rows = p_ref.shape[0]
    weights = (p_ref[...] * (1.0 / push_ref[0])).astype(BF16)
    both = jnp.concatenate([weights, m_ref[...]], axis=0)
    product = jnp.dot(both, ct_ref[...], preferred_element_type=F32)
    y_ref[...] = product[rows:]
    total = local_tokens(r_ref, index, count).astype(F32) + product[:rows]
    s_ref[...] = total
    target = local_tokens(t_ref, index, count).astype(F32)
    add_sums(q_ref, step, total, g_ref[...] * total, target)


def forward(mix, push, lower, upper, params, moment, residual, target, gain, near, pieces):
    rows, width = params.shape
    piece = pieces[0].shape[0]
    count = len(pieces)
    tokens = piece * count
    block = FORWARD_ROWS if rows % FORWARD_ROWS == 0 else 64
    row = lambda n: pl.BlockSpec((block, n), lambda i: (i, 0))
    return pl.pallas_call(
        functools.partial(forward_kernel, count),
        grid=(rows // block,),
        in_specs=[
            SMEM_SPEC,
            SMEM_SPEC,
            whole_spec((8, 128)),
            whole_spec((8, 128)),
            row(width),
            row(width),
            row(tokens),
            row(tokens),
            row(1),
            whole_spec((width, tokens // 2)),
        ]
        + [whole_spec((piece, width))] * count,
        out_specs=[
            row(tokens),
            row(tokens),
            whole_spec((8, tokens)),
            whole_spec((tokens, width)),
            whole_spec((8, 128)),
        ],
        out_shape=[
            jax.ShapeDtypeStruct((rows, tokens), F32),
            jax.ShapeDtypeStruct((rows, tokens), F32),
            jax.ShapeDtypeStruct((8, tokens), F32),
            jax.ShapeDtypeStruct((tokens, width), BF16),
            jax.ShapeDtypeStruct((8, 128), F32),
        ],
        scratch_shapes=[pltpu.VMEM((width, tokens), BF16)],
        compiler_params=params_of(FORWARD_MIB * MIB if tokens <= 512 else 58 * MIB),
        cost_estimate=cost(4 * rows * width * tokens, rows * width * 6),
    )(mix, push, lower, upper, params, moment, residual, target, gain, near, *pieces)


def second_kernel(count, features, push_ref, s_ref, t_ref, g_ref, y_ref, gram_ref, *rest):
    sum_refs, (grad_ref, s2_ref, q_ref, high_ref, low_ref) = rest[:count], rest[count:]
    index = lax.axis_index("fsdp")
    step = pl.program_id(0)

    @pl.when(step == 0)
    def _():
        gram = gram_ref[...]
        high = gram.astype(BF16)
        high_ref[...] = high
        low_ref[...] = (gram - high.astype(F32)).astype(BF16)

    inv, dot = token_stats(sum_refs, features)
    total = s_ref[...]
    target = local_tokens(t_ref, index, count).astype(F32)
    gain = g_ref[...]
    grad = stream_grad(total, target, gain, inv, dot, total.shape[1])
    grad_ref[...] = grad
    moved = jnp.dot(grad, high_ref[...], preferred_element_type=F32)
    moved += jnp.dot(grad, low_ref[...], preferred_element_type=F32)
    total = total - (learn_rate / push_ref[0]) * (beta_decay * y_ref[...] + moved)
    s2_ref[...] = total
    add_sums(q_ref, step, total, gain * total, target)


def second(push, total, target, gain, moment_product, gram, sums, features):
    rows, tokens = total.shape
    count = len(sums)
    block = min(256, rows) if rows % 256 == 0 else min(64, rows)
    row = lambda n: pl.BlockSpec((block, n), lambda i: (i, 0))
    return pl.pallas_call(
        functools.partial(second_kernel, count, features),
        grid=(rows // block,),
        in_specs=[
            SMEM_SPEC,
            row(tokens),
            row(tokens),
            row(1),
            row(tokens),
            pl.BlockSpec((tokens, tokens), lambda i: (0, 0), pipeline_mode=pl.Buffered(1)),
        ]
        + [whole_spec((8, tokens))] * count,
        out_specs=[row(tokens), row(tokens), whole_spec((8, tokens))],
        out_shape=[
            jax.ShapeDtypeStruct((rows, tokens), BF16),
            jax.ShapeDtypeStruct((rows, tokens), F32),
            jax.ShapeDtypeStruct((8, tokens), F32),
        ],
        scratch_shapes=[pltpu.VMEM((tokens, tokens), BF16)] * 2,
        compiler_params=params_of(SECOND_MIB * MIB if tokens <= 512 else 56 * MIB),
        cost_estimate=cost(4 * rows * tokens * tokens, rows * tokens * 16),
    )(push, total, target, gain, moment_product, gram, *sums)


def step_kernel(count, features, has_update, has_final, waits, *refs):
    refs = list(refs)
    take = lambda n: [refs.pop(0) for _ in range(n)]
    (mix_ref,) = take(1)
    if has_update:
        p_in, m_in, grad_ref, s_ref, t_ref, g_ref, c_ref = take(7)
        sum_refs = take(count)
    if has_final:
        master_in, state_in, arrived_ref = take(3)
    take(waits)
    if has_update:
        state_ref, master_ref = take(2)
        inv, dot = token_stats(sum_refs, features)
        target = local_tokens(t_ref, lax.axis_index("fsdp"), count).astype(F32)
        grad2 = stream_grad(s_ref[...], target, g_ref[...], inv, dot, s_ref.shape[1])
        rows = grad2.shape[0]
        both = jnp.dot(
            jnp.concatenate([grad_ref[...], grad2], axis=0),
            c_ref[...],
            preferred_element_type=F32,
        )
        moment = (beta_decay * m_in[...].astype(F32) + both[:rows]).astype(BF16).astype(F32)
        master = p_in[...] - learn_rate * moment
        moment = (beta_decay * moment + both[rows:]).astype(BF16)
        master = master - learn_rate * moment.astype(F32)
        state_ref[0] = master.astype(BF16)
        state_ref[1] = moment
        master_ref[...] = master
    if has_final:
        p_out, m_out = take(2)
        keep, _, _ = shares_of(mix_ref)
        p_out[...] = keep * master_in[...] + arrived_ref[0].astype(F32)
        m_out[...] = (keep * state_in[0].astype(F32) + arrived_ref[1].astype(F32)).astype(BF16)


def step_call(mix, rows, update, done, held, after, features):
    units = rows // UNIT
    operands, specs, out_specs, out_shape = [mix], [SMEM_SPEC], [], []
    count = 0
    flops = nbytes = 0
    if update:
        start, arrays, sums = update
        params, moment, grad, total, target, gain, context = arrays
        width, tokens, count = params.shape[1], total.shape[1], len(sums)
        first = start // UNIT
        row = lambda n: pl.BlockSpec((UNIT, n), lambda i: (first + i, 0))
        operands += [*arrays, *sums]
        specs += [row(width), row(width), row(tokens), row(tokens), row(tokens), row(1)]
        specs += [whole_spec((tokens, width))] + [whole_spec((8, tokens))] * count
        flops += 4 * rows * width * tokens
        nbytes += rows * width * 14
    if done:
        begin, all_rows, master, state, arrived = done
        width = master.shape[1]
        operands += [master, state, arrived]
        specs += [
            pl.BlockSpec((UNIT, width), lambda i: (i, 0)),
            pl.BlockSpec((1, UNIT, width), lambda i: (1, i, 0)),
            pl.BlockSpec((2, UNIT, width), lambda i: (0, i, 0)),
        ]
        nbytes += rows * width * 16
    waits = [*(held if done and held else ()), *after]
    alias = {}
    if done and held:
        alias = {len(operands): 2 if update else 0, len(operands) + 1: 3 if update else 1}
    operands += waits
    specs += [pl.BlockSpec(memory_space=pl.ANY)] * len(waits)
    if update:
        out_specs += [
            pl.BlockSpec((2, UNIT, width), lambda i: (0, i, 0)),
            pl.BlockSpec((UNIT, width), lambda i: (i, 0)),
        ]
        out_shape += [
            jax.ShapeDtypeStruct((2, rows, width), BF16),
            jax.ShapeDtypeStruct((rows, width), F32),
        ]
    if done:
        at = begin // UNIT
        out_specs += [pl.BlockSpec((UNIT, width), lambda i: (at + i, 0))] * 2
        out_shape += [
            jax.ShapeDtypeStruct((all_rows, width), F32),
            jax.ShapeDtypeStruct((all_rows, width), BF16),
        ]
    out = pl.pallas_call(
        functools.partial(
            step_kernel, count, features, bool(update), bool(done), len(waits)
        ),
        grid=(units,),
        in_specs=specs,
        out_specs=out_specs,
        out_shape=out_shape,
        input_output_aliases=alias,
        compiler_params=params_of(STEP_MIB * MIB),
        cost_estimate=cost(flops, nbytes),
    )(*operands)
    made = tuple(out[:2]) if update else None
    return made, tuple(out[-2:]) if done else held


def pair_kernel(mix_ref, master_ref, state_ref, other_ref, *rest):
    out_ref = rest[-1]
    _, mine, theirs = shares_of(mix_ref)
    out_ref[0] = (mine * master_ref[...] + theirs * other_ref[0].astype(F32)).astype(BF16)
    out_ref[1] = (mine * state_ref[0].astype(F32) + theirs * other_ref[1].astype(F32)).astype(BF16)


def pair_sum(mix, master, state, other, after):
    _, rows, width = state.shape
    return pl.pallas_call(
        pair_kernel,
        grid=(rows // UNIT,),
        in_specs=[
            SMEM_SPEC,
            pl.BlockSpec((UNIT, width), lambda i: (i, 0)),
            pl.BlockSpec((1, UNIT, width), lambda i: (1, i, 0)),
            pl.BlockSpec((2, UNIT, width), lambda i: (0, i, 0)),
        ]
        + [pl.BlockSpec(memory_space=pl.ANY)] * len(after),
        out_specs=pl.BlockSpec((2, UNIT, width), lambda i: (0, i, 0)),
        out_shape=jax.ShapeDtypeStruct((2, rows, width), BF16),
        compiler_params=params_of(PAIR_MIB * MIB),
        cost_estimate=cost(6 * rows * width, rows * width * 14),
    )(mix, master, state, other, *after)


def with_partner(value, distance, count):
    return lax.ppermute(value, "fsdp", [(i, i ^ distance) for i in range(count)])


def gather_low(block, count):
    pieces = {0: block}
    distance = count // 4
    while distance:
        for j in list(pieces):
            pieces[j | distance] = with_partner(pieces[j], distance, count)
        distance //= 2
    return [pieces[j] for j in sorted(pieces)]


def all_sums(sums, count):
    return [sums] + [with_partner(sums, m, count) for m in range(1, count)]


def chunk_sizes(rows):
    sizes = []
    for size, part in CHUNKS:
        while sum(sizes) + size <= min(part * rows, rows):
            sizes.append(size)
    while sum(sizes) < rows:
        sizes.append(UNIT)
    return sizes


def local(context, residual, target, norm_gain, params, momentum, push_weight, mix_num):
    count = lax.axis_size("fsdp")
    replicas = lax.axis_size("rep")
    residual, target, params, momentum = residual[0], target[0], params[0], momentum[0]
    rows, width = params.shape
    features = rows * count

    along_z = [(r, (r - 2) % replicas if r % 2 == 0 else (r + 2) % replicas) for r in range(replicas)]
    along_y = [(r, r ^ 1) for r in range(replicas)]
    over_z = lambda value: lax.ppermute(value, "rep", along_z)
    over_y = lambda value: lax.ppermute(value, "rep", along_y)

    far = with_partner(context[0], count // 2, count)
    near_pieces = gather_low(context[0], count)
    push_row = jnp.broadcast_to(push_weight, (8, 128))
    push_lower = lax.ppermute(push_row, "rep", [(r, (r + 1) % replicas) for r in range(replicas)])
    push_upper = lax.ppermute(push_row, "rep", [(r, (r - 1) % replicas) for r in range(replicas)])
    gain = norm_gain[:, None]
    mix = mix_num.reshape(-1)
    near = near_turned(near_pieces, mix, (gain, push_lower, push_upper, momentum, residual, target))
    far, near = lax.optimization_barrier((far, near))
    pieces = near_pieces + gather_low(far, count)
    total, moment_product, sums, tokens_all, new_push = forward(
        mix,
        push_weight,
        push_lower,
        push_upper,
        params,
        momentum,
        residual,
        target,
        gain,
        near,
        pieces,
    )
    sums = all_sums(sums, count)
    gram = lax.dot_general(tokens_all, tokens_all, NT, preferred_element_type=F32)
    grad, total, sums = second(
        push_weight, total, target, gain, moment_product, gram, sums, features
    )
    sums = all_sums(sums, count)

    arrays = (params, momentum, grad, total, target, gain, tokens_all)
    sizes = chunk_sizes(rows)
    chunks = len(sizes)
    starts = [sum(sizes[:c]) for c in range(chunks)]
    made, crossing, arriving = {}, {}, {}
    held = None
    last = ()
    for c in range(-Z_AHEAD, chunks + Y_AHEAD):
        if 0 <= c < chunks:
            state, master = made[c]
            both = pair_sum(mix, master, state, crossing.pop(c), last)
            arriving[c] = over_y(both)
            last = (both,)
        ahead, behind = c + Z_AHEAD, c - Y_AHEAD
        update = (starts[ahead], arrays, sums) if ahead < chunks else None
        done = None
        if behind >= 0:
            state, master = made.pop(behind)
            done = (starts[behind], rows, master, state, arriving.pop(behind))
        if update and done and sizes[ahead] == sizes[behind]:
            calls = [(sizes[ahead], update, done)]
        else:
            calls = [(sizes[ahead], update, None)] if update else []
            calls += [(sizes[behind], None, done)] if done else []
        for size, update, done in calls:
            out, held = step_call(mix, size, update, done, held, last, features)
            if out:
                made[ahead] = out
                crossing[ahead] = over_z(out[0])
                last = (out[0],)
    return (held[0][None], held[1][None], new_push[0, 0:1])


def solution(mesh):
    return jax.shard_map(
        local,
        mesh=mesh,
        in_specs=(
            P("rep", "fsdp", None),
            P("rep", "fsdp", None),
            P("rep", "fsdp", None),
            P("fsdp"),
            P("rep", "fsdp", None),
            P("rep", "fsdp", None),
            P("rep"),
            P(),
        ),
        out_specs=(P("rep", "fsdp", None), P("rep", "fsdp", None), P("rep")),
        check_vma=False,
    )
```

```python
import functools

import jax
import jax.numpy as jnp
from jax import lax
from jax.experimental import pallas as pl
from jax.experimental.pallas import tpu as pltpu
from jax.sharding import PartitionSpec as P

epsilon = 1e-05
learn_rate = 0.5
beta_decay = 0.9

UNIT = 64
CHUNKS = ((64, 1),)
Z_AHEAD = 2
Y_AHEAD = 1
MIB = 1024 * 1024
FORWARD_ROWS = 256
FORWARD_MIB = SECOND_MIB = 24
STEP_MIB = PAIR_MIB = 44
F32 = jnp.float32
BF16 = jnp.bfloat16
NT = (((1,), (1,)), ((), ()))

SMEM_SPEC = pl.BlockSpec(memory_space=pltpu.SMEM)


def whole_spec(shape):
    return pl.BlockSpec(shape, lambda i: (0,) * len(shape))


def params_of(limit):
    return pltpu.CompilerParams(
        dimension_semantics=("arbitrary",), vmem_limit_bytes=limit
    )


def cost(flops, nbytes):
    return pl.CostEstimate(flops=flops, bytes_accessed=nbytes, transcendentals=0)


def shares_of(mix_ref):
    replicas = mix_ref.shape[0] // 3
    replica = lax.axis_index("rep")
    odd = lax.rem(replica, 2)
    away = lax.rem(replica + jnp.where(odd == 1, replicas - 2, 2), replicas)

    def share(at, column):
        row = [mix_ref[3 * at + k].astype(F32) for k in range(3)]
        return mix_ref[3 * at + column].astype(F32) / (row[0] + row[1] + row[2])

    return share(replica, 0), share(replica, 2 - odd), share(away, 1 + odd)


def neighbour_shares(mix_ref):
    replicas = mix_ref.shape[0] // 3
    replica = lax.axis_index("rep")

    def share(at, column):
        row = [mix_ref[3 * at + k].astype(F32) for k in range(3)]
        return row[column] / (row[0] + row[1] + row[2])

    lower = lax.rem(replica + replicas - 1, replicas)
    upper = lax.rem(replica + 1, replicas)
    return share(replica, 0), share(lower, 2), share(upper, 1)


def local_tokens(ref, index, count):
    width = ref.shape[1] // count
    blocks = [
        ref[:, pl.ds(pl.multiple_of(lax.bitwise_xor(index, j) * width, width), width)]
        for j in range(count)
    ]
    return jnp.concatenate(blocks, axis=1)


def add_sums(sums_ref, step, total, scaled, target):
    parts = jnp.concatenate(
        [
            jnp.sum(total * total, axis=0, keepdims=True),
            jnp.sum(scaled * scaled, axis=0, keepdims=True),
            jnp.sum(scaled * target, axis=0, keepdims=True),
            jnp.zeros((5, total.shape[1]), F32),
        ],
        axis=0,
    )

    @pl.when(step == 0)
    def _():
        sums_ref[...] = parts

    @pl.when(step > 0)
    def _():
        sums_ref[...] += parts


def token_stats(sum_refs, features):
    count = len(sum_refs)
    tokens = sum_refs[0].shape[1]
    width = tokens // count
    full = sum_refs[0][...]
    for m in range(1, count):
        other = sum_refs[m]
        full = full + jnp.concatenate(
            [other[:, (j ^ m) * width : ((j ^ m) + 1) * width] for j in range(count)],
            axis=1,
        )
    inv = lax.rsqrt(full[0:1] / features + epsilon)
    dot = (inv * full[1:2] - full[2:3]) / (tokens * features)
    return inv, dot


def stream_grad(total, target, gain, inv, dot, tokens):
    scaled = gain * ((gain * total * inv - target) / tokens)
    return (scaled * inv - total * (inv * inv * inv * dot)).astype(BF16)


def transpose_pieces(piece_refs, out_ref):
    width = piece_refs[0].shape[0]
    for j, piece in enumerate(piece_refs):
        out_ref[:, j * width : (j + 1) * width] = piece[...].T


def near_kernel(count, *refs):
    transpose_pieces(refs[:count], refs[-1])


def near_turned(pieces, mix, beside):
    piece, width = pieces[0].shape
    tokens = piece * len(pieces)
    return pl.pallas_call(
        functools.partial(near_kernel, len(pieces)),
        grid=(1,),
        in_specs=[whole_spec((piece, width))] * len(pieces)
        + [SMEM_SPEC]
        + [pl.BlockSpec(memory_space=pl.ANY)] * len(beside),
        out_specs=whole_spec((width, tokens)),
        out_shape=jax.ShapeDtypeStruct((width, tokens), BF16),
        compiler_params=params_of(FORWARD_MIB * MIB),
        cost_estimate=cost(2 * tokens * width, 4 * tokens * width),
    )(*pieces, mix, *beside)


def forward_kernel(
    count, mix_ref, push_ref, low_ref, high_ref, p_ref, m_ref, r_ref, t_ref, g_ref, near_ref, *rest
):
    pieces, (s_ref, y_ref, q_ref, c_ref, push_out, ct_ref) = rest[:count], rest[count:]
    index = lax.axis_index("fsdp")
    step = pl.program_id(0)

    @pl.when(step == 0)
    def _():
        half = near_ref.shape[1]
        ct_ref[:, :half] = near_ref[...]
        transpose_pieces(pieces[count // 2 :], ct_ref.at[:, half:])
        width = pieces[0].shape[0]
        for j, piece in enumerate(pieces):
            c_ref[j * width : (j + 1) * width, :] = piece[...]
        keep, lower, upper = neighbour_shares(mix_ref)
        push_out[...] = keep * push_ref[0] + lower * low_ref[...] + upper * high_ref[...]

    rows = p_ref.shape[0]
    weights = (p_ref[...] * (1.0 / push_ref[0])).astype(BF16)
    both = jnp.concatenate([weights, m_ref[...]], axis=0)
    product = jnp.dot(both, ct_ref[...], preferred_element_type=F32)
    y_ref[...] = product[rows:]
    total = local_tokens(r_ref, index, count).astype(F32) + product[:rows]
    s_ref[...] = total
    target = local_tokens(t_ref, index, count).astype(F32)
    add_sums(q_ref, step, total, g_ref[...] * total, target)


def forward(mix, push, lower, upper, params, moment, residual, target, gain, near, pieces):
    rows, width = params.shape
    piece = pieces[0].shape[0]
    count = len(pieces)
    tokens = piece * count
    block = FORWARD_ROWS if rows % FORWARD_ROWS == 0 else 64
    row = lambda n: pl.BlockSpec((block, n), lambda i: (i, 0))
    return pl.pallas_call(
        functools.partial(forward_kernel, count),
        grid=(rows // block,),
        in_specs=[
            SMEM_SPEC,
            SMEM_SPEC,
            whole_spec((8, 128)),
            whole_spec((8, 128)),
            row(width),
            row(width),
            row(tokens),
            row(tokens),
            row(1),
            whole_spec((width, tokens // 2)),
        ]
        + [whole_spec((piece, width))] * count,
        out_specs=[
            row(tokens),
            row(tokens),
            whole_spec((8, tokens)),
            whole_spec((tokens, width)),
            whole_spec((8, 128)),
        ],
        out_shape=[
            jax.ShapeDtypeStruct((rows, tokens), F32),
            jax.ShapeDtypeStruct((rows, tokens), F32),
            jax.ShapeDtypeStruct((8, tokens), F32),
            jax.ShapeDtypeStruct((tokens, width), BF16),
            jax.ShapeDtypeStruct((8, 128), F32),
        ],
        scratch_shapes=[pltpu.VMEM((width, tokens), BF16)],
        compiler_params=params_of(FORWARD_MIB * MIB if tokens <= 512 else 58 * MIB),
        cost_estimate=cost(4 * rows * width * tokens, rows * width * 6),
    )(mix, push, lower, upper, params, moment, residual, target, gain, near, *pieces)


def second_kernel(count, features, push_ref, s_ref, t_ref, g_ref, y_ref, gram_ref, *rest):
    sum_refs, (grad_ref, s2_ref, q_ref, high_ref, low_ref) = rest[:count], rest[count:]
    index = lax.axis_index("fsdp")
    step = pl.program_id(0)

    @pl.when(step == 0)
    def _():
        gram = gram_ref[...]
        high = gram.astype(BF16)
        high_ref[...] = high
        low_ref[...] = (gram - high.astype(F32)).astype(BF16)

    inv, dot = token_stats(sum_refs, features)
    total = s_ref[...]
    target = local_tokens(t_ref, index, count).astype(F32)
    gain = g_ref[...]
    grad = stream_grad(total, target, gain, inv, dot, total.shape[1])
    grad_ref[...] = grad
    moved = jnp.dot(grad, high_ref[...], preferred_element_type=F32)
    moved += jnp.dot(grad, low_ref[...], preferred_element_type=F32)
    total = total - (learn_rate / push_ref[0]) * (beta_decay * y_ref[...] + moved)
    s2_ref[...] = total
    add_sums(q_ref, step, total, gain * total, target)


def second(push, total, target, gain, moment_product, gram, sums, features):
    rows, tokens = total.shape
    count = len(sums)
    block = min(256, rows) if rows % 256 == 0 else min(64, rows)
    row = lambda n: pl.BlockSpec((block, n), lambda i: (i, 0))
    return pl.pallas_call(
        functools.partial(second_kernel, count, features),
        grid=(rows // block,),
        in_specs=[
            SMEM_SPEC,
            row(tokens),
            row(tokens),
            row(1),
            row(tokens),
            pl.BlockSpec((tokens, tokens), lambda i: (0, 0), pipeline_mode=pl.Buffered(1)),
        ]
        + [whole_spec((8, tokens))] * count,
        out_specs=[row(tokens), row(tokens), whole_spec((8, tokens))],
        out_shape=[
            jax.ShapeDtypeStruct((rows, tokens), BF16),
            jax.ShapeDtypeStruct((rows, tokens), F32),
            jax.ShapeDtypeStruct((8, tokens), F32),
        ],
        scratch_shapes=[pltpu.VMEM((tokens, tokens), BF16)] * 2,
        compiler_params=params_of(SECOND_MIB * MIB if tokens <= 512 else 56 * MIB),
        cost_estimate=cost(4 * rows * tokens * tokens, rows * tokens * 16),
    )(push, total, target, gain, moment_product, gram, *sums)


def step_kernel(count, features, has_update, has_final, waits, *refs):
    refs = list(refs)
    take = lambda n: [refs.pop(0) for _ in range(n)]
    (mix_ref,) = take(1)
    if has_update:
        p_in, m_in, grad_ref, s_ref, t_ref, g_ref, c_ref = take(7)
        sum_refs = take(count)
    if has_final:
        master_in, state_in, arrived_ref = take(3)
    take(waits)
    if has_update:
        state_ref, master_ref = take(2)
        inv, dot = token_stats(sum_refs, features)
        target = local_tokens(t_ref, lax.axis_index("fsdp"), count).astype(F32)
        grad2 = stream_grad(s_ref[...], target, g_ref[...], inv, dot, s_ref.shape[1])
        rows = grad2.shape[0]
        both = jnp.dot(
            jnp.concatenate([grad_ref[...], grad2], axis=0),
            c_ref[...],
            preferred_element_type=F32,
        )
        moment = (beta_decay * m_in[...].astype(F32) + both[:rows]).astype(BF16).astype(F32)
        master = p_in[...] - learn_rate * moment
        moment = (beta_decay * moment + both[rows:]).astype(BF16)
        master = master - learn_rate * moment.astype(F32)
        state_ref[0] = master.astype(BF16)
        state_ref[1] = moment
        master_ref[...] = master
    if has_final:
        p_out, m_out = take(2)
        keep, _, _ = shares_of(mix_ref)
        p_out[...] = keep * master_in[...] + arrived_ref[0].astype(F32)
        m_out[...] = (keep * state_in[0].astype(F32) + arrived_ref[1].astype(F32)).astype(BF16)


def step_call(mix, rows, update, done, held, after, features):
    units = rows // UNIT
    operands, specs, out_specs, out_shape = [mix], [SMEM_SPEC], [], []
    count = 0
    flops = nbytes = 0
    if update:
        start, arrays, sums = update
        params, moment, grad, total, target, gain, context = arrays
        width, tokens, count = params.shape[1], total.shape[1], len(sums)
        first = start // UNIT
        row = lambda n: pl.BlockSpec((UNIT, n), lambda i: (first + i, 0))
        operands += [*arrays, *sums]
        specs += [row(width), row(width), row(tokens), row(tokens), row(tokens), row(1)]
        specs += [whole_spec((tokens, width))] + [whole_spec((8, tokens))] * count
        flops += 4 * rows * width * tokens
        nbytes += rows * width * 14
    if done:
        begin, all_rows, master, state, arrived = done
        width = master.shape[1]
        operands += [master, state, arrived]
        specs += [
            pl.BlockSpec((UNIT, width), lambda i: (i, 0)),
            pl.BlockSpec((1, UNIT, width), lambda i: (1, i, 0)),
            pl.BlockSpec((2, UNIT, width), lambda i: (0, i, 0)),
        ]
        nbytes += rows * width * 16
    waits = [*(held if done and held else ()), *after]
    alias = {}
    if done and held:
        alias = {len(operands): 2 if update else 0, len(operands) + 1: 3 if update else 1}
    operands += waits
    specs += [pl.BlockSpec(memory_space=pl.ANY)] * len(waits)
    if update:
        out_specs += [
            pl.BlockSpec((2, UNIT, width), lambda i: (0, i, 0)),
            pl.BlockSpec((UNIT, width), lambda i: (i, 0)),
        ]
        out_shape += [
            jax.ShapeDtypeStruct((2, rows, width), BF16),
            jax.ShapeDtypeStruct((rows, width), F32),
        ]
    if done:
        at = begin // UNIT
        out_specs += [pl.BlockSpec((UNIT, width), lambda i: (at + i, 0))] * 2
        out_shape += [
            jax.ShapeDtypeStruct((all_rows, width), F32),
            jax.ShapeDtypeStruct((all_rows, width), BF16),
        ]
    out = pl.pallas_call(
        functools.partial(
            step_kernel, count, features, bool(update), bool(done), len(waits)
        ),
        grid=(units,),
        in_specs=specs,
        out_specs=out_specs,
        out_shape=out_shape,
        input_output_aliases=alias,
        compiler_params=params_of(STEP_MIB * MIB),
        cost_estimate=cost(flops, nbytes),
    )(*operands)
    made = tuple(out[:2]) if update else None
    return made, tuple(out[-2:]) if done else held


def pair_kernel(mix_ref, master_ref, state_ref, other_ref, *rest):
    out_ref = rest[-1]
    _, mine, theirs = shares_of(mix_ref)
    out_ref[0] = (mine * master_ref[...] + theirs * other_ref[0].astype(F32)).astype(BF16)
    out_ref[1] = (mine * state_ref[0].astype(F32) + theirs * other_ref[1].astype(F32)).astype(BF16)


def pair_sum(mix, master, state, other, after):
    _, rows, width = state.shape
    return pl.pallas_call(
        pair_kernel,
        grid=(rows // UNIT,),
        in_specs=[
            SMEM_SPEC,
            pl.BlockSpec((UNIT, width), lambda i: (i, 0)),
            pl.BlockSpec((1, UNIT, width), lambda i: (1, i, 0)),
            pl.BlockSpec((2, UNIT, width), lambda i: (0, i, 0)),
        ]
        + [pl.BlockSpec(memory_space=pl.ANY)] * len(after),
        out_specs=pl.BlockSpec((2, UNIT, width), lambda i: (0, i, 0)),
        out_shape=jax.ShapeDtypeStruct((2, rows, width), BF16),
        compiler_params=params_of(PAIR_MIB * MIB),
        cost_estimate=cost(6 * rows * width, rows * width * 14),
    )(mix, master, state, other, *after)


def with_partner(value, distance, count):
    return lax.ppermute(value, "fsdp", [(i, i ^ distance) for i in range(count)])


def gather_low(block, count):
    pieces = {0: block}
    distance = count // 4
    while distance:
        for j in list(pieces):
            pieces[j | distance] = with_partner(pieces[j], distance, count)
        distance //= 2
    return [pieces[j] for j in sorted(pieces)]


def all_sums(sums, count):
    return [sums] + [with_partner(sums, m, count) for m in range(1, count)]


def chunk_sizes(rows):
    sizes = []
    for size, part in CHUNKS:
        while sum(sizes) + size <= min(part * rows, rows):
            sizes.append(size)
    while sum(sizes) < rows:
        sizes.append(UNIT)
    return sizes


def local(context, residual, target, norm_gain, params, momentum, push_weight, mix_num):
    count = lax.axis_size("fsdp")
    replicas = lax.axis_size("rep")
    residual, target, params, momentum = residual[0], target[0], params[0], momentum[0]
    rows, width = params.shape
    features = rows * count

    along_z = [(r, (r - 2) % replicas if r % 2 == 0 else (r + 2) % replicas) for r in range(replicas)]
    along_y = [(r, r ^ 1) for r in range(replicas)]
    over_z = lambda value: lax.ppermute(value, "rep", along_z)
    over_y = lambda value: lax.ppermute(value, "rep", along_y)

    far = with_partner(context[0], count // 2, count)
    near_pieces = gather_low(context[0], count)
    push_row = jnp.broadcast_to(push_weight, (8, 128))
    push_lower = lax.ppermute(push_row, "rep", [(r, (r + 1) % replicas) for r in range(replicas)])
    push_upper = lax.ppermute(push_row, "rep", [(r, (r - 1) % replicas) for r in range(replicas)])
    gain = norm_gain[:, None]
    mix = mix_num.reshape(-1)
    near = near_turned(near_pieces, mix, (gain, push_lower, push_upper, momentum, residual, target))
    far, near = lax.optimization_barrier((far, near))
    pieces = near_pieces + gather_low(far, count)
    total, moment_product, sums, tokens_all, new_push = forward(
        mix,
        push_weight,
        push_lower,
        push_upper,
        params,
        momentum,
        residual,
        target,
        gain,
        near,
        pieces,
    )
    sums = all_sums(sums, count)
    gram = lax.dot_general(tokens_all, tokens_all, NT, preferred_element_type=F32)
    grad, total, sums = second(
        push_weight, total, target, gain, moment_product, gram, sums, features
    )
    sums = all_sums(sums, count)

    arrays = (params, momentum, grad, total, target, gain, tokens_all)
    sizes = chunk_sizes(rows)
    chunks = len(sizes)
    starts = [sum(sizes[:c]) for c in range(chunks)]
    made, crossing, arriving = {}, {}, {}
    held = None
    last = ()
    for c in range(-Z_AHEAD, chunks + Y_AHEAD):
        if 0 <= c < chunks:
            state, master = made[c]
            both = pair_sum(mix, master, state, crossing.pop(c), last)
            arriving[c] = over_y(both)
            last = (both,)
        ahead, behind = c + Z_AHEAD, c - Y_AHEAD
        update = (starts[ahead], arrays, sums) if ahead < chunks else None
        done = None
        if behind >= 0:
            state, master = made.pop(behind)
            done = (starts[behind], rows, master, state, arriving.pop(behind))
        if update and done and sizes[ahead] == sizes[behind]:
            calls = [(sizes[ahead], update, done)]
        else:
            calls = [(sizes[ahead], update, None)] if update else []
            calls += [(sizes[behind], None, done)] if done else []
        for size, update, done in calls:
            out, held = step_call(mix, size, update, done, held, last, features)
            if out:
                made[ahead] = out
                crossing[ahead] = over_z(out[0])
                last = (out[0],)
    return (held[0][None], held[1][None], new_push[0, 0:1])


def solution(mesh):
    return jax.shard_map(
        local,
        mesh=mesh,
        in_specs=(
            P("rep", "fsdp", None),
            P("rep", "fsdp", None),
            P("rep", "fsdp", None),
            P("fsdp"),
            P("rep", "fsdp", None),
            P("rep", "fsdp", None),
            P("rep"),
            P(),
        ),
        out_specs=(P("rep", "fsdp", None), P("rep", "fsdp", None), P("rep")),
        check_vma=False,
    )
```

```python
import functools

import jax
import jax.numpy as jnp
from jax import lax
from jax.experimental import pallas as pl
from jax.experimental.pallas import tpu as pltpu
from jax.sharding import PartitionSpec as P

epsilon = 1e-05
learn_rate = 0.5
beta_decay = 0.9

UNIT = 64
CHUNKS = ((64, 1),)
Z_AHEAD = 2
Y_AHEAD = 1
MIB = 1024 * 1024
FORWARD_ROWS = 256
FORWARD_MIB = SECOND_MIB = 24
STEP_MIB = PAIR_MIB = 38
F32 = jnp.float32
BF16 = jnp.bfloat16
NT = (((1,), (1,)), ((), ()))

SMEM_SPEC = pl.BlockSpec(memory_space=pltpu.SMEM)


def whole_spec(shape):
    return pl.BlockSpec(shape, lambda i: (0,) * len(shape))


def params_of(limit):
    return pltpu.CompilerParams(
        dimension_semantics=("arbitrary",), vmem_limit_bytes=limit
    )


def cost(flops, nbytes):
    return pl.CostEstimate(flops=flops, bytes_accessed=nbytes, transcendentals=0)


def shares_of(mix_ref):
    replicas = mix_ref.shape[0] // 3
    replica = lax.axis_index("rep")
    odd = lax.rem(replica, 2)
    away = lax.rem(replica + jnp.where(odd == 1, replicas - 2, 2), replicas)

    def share(at, column):
        row = [mix_ref[3 * at + k].astype(F32) for k in range(3)]
        return mix_ref[3 * at + column].astype(F32) / (row[0] + row[1] + row[2])

    return share(replica, 0), share(replica, 2 - odd), share(away, 1 + odd)


def neighbour_shares(mix_ref):
    replicas = mix_ref.shape[0] // 3
    replica = lax.axis_index("rep")

    def share(at, column):
        row = [mix_ref[3 * at + k].astype(F32) for k in range(3)]
        return row[column] / (row[0] + row[1] + row[2])

    lower = lax.rem(replica + replicas - 1, replicas)
    upper = lax.rem(replica + 1, replicas)
    return share(replica, 0), share(lower, 2), share(upper, 1)


def local_tokens(ref, index, count):
    width = ref.shape[1] // count
    blocks = [
        ref[:, pl.ds(pl.multiple_of(lax.bitwise_xor(index, j) * width, width), width)]
        for j in range(count)
    ]
    return jnp.concatenate(blocks, axis=1)


def add_sums(sums_ref, step, total, scaled, target):
    parts = jnp.concatenate(
        [
            jnp.sum(total * total, axis=0, keepdims=True),
            jnp.sum(scaled * scaled, axis=0, keepdims=True),
            jnp.sum(scaled * target, axis=0, keepdims=True),
            jnp.zeros((5, total.shape[1]), F32),
        ],
        axis=0,
    )

    @pl.when(step == 0)
    def _():
        sums_ref[...] = parts

    @pl.when(step > 0)
    def _():
        sums_ref[...] += parts


def token_stats(sum_refs, features):
    count = len(sum_refs)
    tokens = sum_refs[0].shape[1]
    width = tokens // count
    full = sum_refs[0][...]
    for m in range(1, count):
        other = sum_refs[m]
        full = full + jnp.concatenate(
            [other[:, (j ^ m) * width : ((j ^ m) + 1) * width] for j in range(count)],
            axis=1,
        )
    inv = lax.rsqrt(full[0:1] / features + epsilon)
    dot = (inv * full[1:2] - full[2:3]) / (tokens * features)
    return inv, dot


def stream_grad(total, target, gain, inv, dot, tokens):
    scaled = gain * ((gain * total * inv - target) / tokens)
    return (scaled * inv - total * (inv * inv * inv * dot)).astype(BF16)


def transpose_pieces(piece_refs, out_ref):
    width = piece_refs[0].shape[0]
    for j, piece in enumerate(piece_refs):
        out_ref[:, j * width : (j + 1) * width] = piece[...].T


def near_kernel(count, *refs):
    transpose_pieces(refs[:count], refs[-1])


def near_turned(pieces, mix, beside):
    piece, width = pieces[0].shape
    tokens = piece * len(pieces)
    return pl.pallas_call(
        functools.partial(near_kernel, len(pieces)),
        grid=(1,),
        in_specs=[whole_spec((piece, width))] * len(pieces)
        + [SMEM_SPEC]
        + [pl.BlockSpec(memory_space=pl.ANY)] * len(beside),
        out_specs=whole_spec((width, tokens)),
        out_shape=jax.ShapeDtypeStruct((width, tokens), BF16),
        compiler_params=params_of(FORWARD_MIB * MIB),
        cost_estimate=cost(2 * tokens * width, 4 * tokens * width),
    )(*pieces, mix, *beside)


def forward_kernel(
    count, mix_ref, push_ref, low_ref, high_ref, p_ref, m_ref, r_ref, t_ref, g_ref, near_ref, *rest
):
    pieces, (s_ref, y_ref, q_ref, c_ref, push_out, ct_ref) = rest[:count], rest[count:]
    index = lax.axis_index("fsdp")
    step = pl.program_id(0)

    @pl.when(step == 0)
    def _():
        half = near_ref.shape[1]
        ct_ref[:, :half] = near_ref[...]
        transpose_pieces(pieces[count // 2 :], ct_ref.at[:, half:])
        width = pieces[0].shape[0]
        for j, piece in enumerate(pieces):
            c_ref[j * width : (j + 1) * width, :] = piece[...]
        keep, lower, upper = neighbour_shares(mix_ref)
        push_out[...] = keep * push_ref[0] + lower * low_ref[...] + upper * high_ref[...]

    rows = p_ref.shape[0]
    weights = (p_ref[...] * (1.0 / push_ref[0])).astype(BF16)
    both = jnp.concatenate([weights, m_ref[...]], axis=0)
    product = jnp.dot(both, ct_ref[...], preferred_element_type=F32)
    y_ref[...] = product[rows:]
    total = local_tokens(r_ref, index, count).astype(F32) + product[:rows]
    s_ref[...] = total
    target = local_tokens(t_ref, index, count).astype(F32)
    add_sums(q_ref, step, total, g_ref[...] * total, target)


def forward(mix, push, lower, upper, params, moment, residual, target, gain, near, pieces):
    rows, width = params.shape
    piece = pieces[0].shape[0]
    count = len(pieces)
    tokens = piece * count
    block = FORWARD_ROWS if rows % FORWARD_ROWS == 0 else 64
    row = lambda n: pl.BlockSpec((block, n), lambda i: (i, 0))
    return pl.pallas_call(
        functools.partial(forward_kernel, count),
        grid=(rows // block,),
        in_specs=[
            SMEM_SPEC,
            SMEM_SPEC,
            whole_spec((8, 128)),
            whole_spec((8, 128)),
            row(width),
            row(width),
            row(tokens),
            row(tokens),
            row(1),
            whole_spec((width, tokens // 2)),
        ]
        + [whole_spec((piece, width))] * count,
        out_specs=[
            row(tokens),
            row(tokens),
            whole_spec((8, tokens)),
            whole_spec((tokens, width)),
            whole_spec((8, 128)),
        ],
        out_shape=[
            jax.ShapeDtypeStruct((rows, tokens), F32),
            jax.ShapeDtypeStruct((rows, tokens), F32),
            jax.ShapeDtypeStruct((8, tokens), F32),
            jax.ShapeDtypeStruct((tokens, width), BF16),
            jax.ShapeDtypeStruct((8, 128), F32),
        ],
        scratch_shapes=[pltpu.VMEM((width, tokens), BF16)],
        compiler_params=params_of(FORWARD_MIB * MIB if tokens <= 512 else 58 * MIB),
        cost_estimate=cost(4 * rows * width * tokens, rows * width * 6),
    )(mix, push, lower, upper, params, moment, residual, target, gain, near, *pieces)


def second_kernel(count, features, push_ref, s_ref, t_ref, g_ref, y_ref, gram_ref, *rest):
    sum_refs, (grad_ref, s2_ref, q_ref, high_ref, low_ref) = rest[:count], rest[count:]
    index = lax.axis_index("fsdp")
    step = pl.program_id(0)

    @pl.when(step == 0)
    def _():
        gram = gram_ref[...]
        high = gram.astype(BF16)
        high_ref[...] = high
        low_ref[...] = (gram - high.astype(F32)).astype(BF16)

    inv, dot = token_stats(sum_refs, features)
    total = s_ref[...]
    target = local_tokens(t_ref, index, count).astype(F32)
    gain = g_ref[...]
    grad = stream_grad(total, target, gain, inv, dot, total.shape[1])
    grad_ref[...] = grad
    moved = jnp.dot(grad, high_ref[...], preferred_element_type=F32)
    moved += jnp.dot(grad, low_ref[...], preferred_element_type=F32)
    total = total - (learn_rate / push_ref[0]) * (beta_decay * y_ref[...] + moved)
    s2_ref[...] = total
    add_sums(q_ref, step, total, gain * total, target)


def second(push, total, target, gain, moment_product, gram, sums, features):
    rows, tokens = total.shape
    count = len(sums)
    block = min(256, rows) if rows % 256 == 0 else min(64, rows)
    row = lambda n: pl.BlockSpec((block, n), lambda i: (i, 0))
    return pl.pallas_call(
        functools.partial(second_kernel, count, features),
        grid=(rows // block,),
        in_specs=[
            SMEM_SPEC,
            row(tokens),
            row(tokens),
            row(1),
            row(tokens),
            pl.BlockSpec((tokens, tokens), lambda i: (0, 0), pipeline_mode=pl.Buffered(1)),
        ]
        + [whole_spec((8, tokens))] * count,
        out_specs=[row(tokens), row(tokens), whole_spec((8, tokens))],
        out_shape=[
            jax.ShapeDtypeStruct((rows, tokens), BF16),
            jax.ShapeDtypeStruct((rows, tokens), F32),
            jax.ShapeDtypeStruct((8, tokens), F32),
        ],
        scratch_shapes=[pltpu.VMEM((tokens, tokens), BF16)] * 2,
        compiler_params=params_of(SECOND_MIB * MIB if tokens <= 512 else 56 * MIB),
        cost_estimate=cost(4 * rows * tokens * tokens, rows * tokens * 16),
    )(push, total, target, gain, moment_product, gram, *sums)


def step_kernel(count, features, has_update, has_final, waits, *refs):
    refs = list(refs)
    take = lambda n: [refs.pop(0) for _ in range(n)]
    (mix_ref,) = take(1)
    if has_update:
        p_in, m_in, grad_ref, s_ref, t_ref, g_ref, c_ref = take(7)
        sum_refs = take(count)
    if has_final:
        master_in, state_in, arrived_ref = take(3)
    take(waits)
    if has_update:
        state_ref, master_ref = take(2)
        inv, dot = token_stats(sum_refs, features)
        target = local_tokens(t_ref, lax.axis_index("fsdp"), count).astype(F32)
        grad2 = stream_grad(s_ref[...], target, g_ref[...], inv, dot, s_ref.shape[1])
        rows = grad2.shape[0]
        both = jnp.dot(
            jnp.concatenate([grad_ref[...], grad2], axis=0),
            c_ref[...],
            preferred_element_type=F32,
        )
        moment = (beta_decay * m_in[...].astype(F32) + both[:rows]).astype(BF16).astype(F32)
        master = p_in[...] - learn_rate * moment
        moment = (beta_decay * moment + both[rows:]).astype(BF16)
        master = master - learn_rate * moment.astype(F32)
        state_ref[0] = master.astype(BF16)
        state_ref[1] = moment
        master_ref[...] = master
    if has_final:
        p_out, m_out = take(2)
        keep, _, _ = shares_of(mix_ref)
        p_out[...] = keep * master_in[...] + arrived_ref[0].astype(F32)
        m_out[...] = (keep * state_in[0].astype(F32) + arrived_ref[1].astype(F32)).astype(BF16)


def step_call(mix, rows, update, done, held, after, features):
    units = rows // UNIT
    operands, specs, out_specs, out_shape = [mix], [SMEM_SPEC], [], []
    count = 0
    flops = nbytes = 0
    if update:
        start, arrays, sums = update
        params, moment, grad, total, target, gain, context = arrays
        width, tokens, count = params.shape[1], total.shape[1], len(sums)
        first = start // UNIT
        row = lambda n: pl.BlockSpec((UNIT, n), lambda i: (first + i, 0))
        operands += [*arrays, *sums]
        specs += [row(width), row(width), row(tokens), row(tokens), row(tokens), row(1)]
        specs += [whole_spec((tokens, width))] + [whole_spec((8, tokens))] * count
        flops += 4 * rows * width * tokens
        nbytes += rows * width * 14
    if done:
        begin, all_rows, master, state, arrived = done
        width = master.shape[1]
        operands += [master, state, arrived]
        specs += [
            pl.BlockSpec((UNIT, width), lambda i: (i, 0)),
            pl.BlockSpec((1, UNIT, width), lambda i: (1, i, 0)),
            pl.BlockSpec((2, UNIT, width), lambda i: (0, i, 0)),
        ]
        nbytes += rows * width * 16
    waits = [*(held if done and held else ()), *after]
    alias = {}
    if done and held:
        alias = {len(operands): 2 if update else 0, len(operands) + 1: 3 if update else 1}
    operands += waits
    specs += [pl.BlockSpec(memory_space=pl.ANY)] * len(waits)
    if update:
        out_specs += [
            pl.BlockSpec((2, UNIT, width), lambda i: (0, i, 0)),
            pl.BlockSpec((UNIT, width), lambda i: (i, 0)),
        ]
        out_shape += [
            jax.ShapeDtypeStruct((2, rows, width), BF16),
            jax.ShapeDtypeStruct((rows, width), F32),
        ]
    if done:
        at = begin // UNIT
        out_specs += [pl.BlockSpec((UNIT, width), lambda i: (at + i, 0))] * 2
        out_shape += [
            jax.ShapeDtypeStruct((all_rows, width), F32),
            jax.ShapeDtypeStruct((all_rows, width), BF16),
        ]
    out = pl.pallas_call(
        functools.partial(
            step_kernel, count, features, bool(update), bool(done), len(waits)
        ),
        grid=(units,),
        in_specs=specs,
        out_specs=out_specs,
        out_shape=out_shape,
        input_output_aliases=alias,
        compiler_params=params_of(STEP_MIB * MIB),
        cost_estimate=cost(flops, nbytes),
    )(*operands)
    made = tuple(out[:2]) if update else None
    return made, tuple(out[-2:]) if done else held


def pair_kernel(mix_ref, master_ref, state_ref, other_ref, *rest):
    out_ref = rest[-1]
    _, mine, theirs = shares_of(mix_ref)
    out_ref[0] = (mine * master_ref[...] + theirs * other_ref[0].astype(F32)).astype(BF16)
    out_ref[1] = (mine * state_ref[0].astype(F32) + theirs * other_ref[1].astype(F32)).astype(BF16)


def pair_sum(mix, master, state, other, after):
    _, rows, width = state.shape
    return pl.pallas_call(
        pair_kernel,
        grid=(rows // UNIT,),
        in_specs=[
            SMEM_SPEC,
            pl.BlockSpec((UNIT, width), lambda i: (i, 0)),
            pl.BlockSpec((1, UNIT, width), lambda i: (1, i, 0)),
            pl.BlockSpec((2, UNIT, width), lambda i: (0, i, 0)),
        ]
        + [pl.BlockSpec(memory_space=pl.ANY)] * len(after),
        out_specs=pl.BlockSpec((2, UNIT, width), lambda i: (0, i, 0)),
        out_shape=jax.ShapeDtypeStruct((2, rows, width), BF16),
        compiler_params=params_of(PAIR_MIB * MIB),
        cost_estimate=cost(6 * rows * width, rows * width * 14),
    )(mix, master, state, other, *after)


def with_partner(value, distance, count):
    return lax.ppermute(value, "fsdp", [(i, i ^ distance) for i in range(count)])


def gather_low(block, count):
    pieces = {0: block}
    distance = count // 4
    while distance:
        for j in list(pieces):
            pieces[j | distance] = with_partner(pieces[j], distance, count)
        distance //= 2
    return [pieces[j] for j in sorted(pieces)]


def all_sums(sums, count):
    return [sums] + [with_partner(sums, m, count) for m in range(1, count)]


def chunk_sizes(rows):
    sizes = []
    for size, part in CHUNKS:
        while sum(sizes) + size <= min(part * rows, rows):
            sizes.append(size)
    while sum(sizes) < rows:
        sizes.append(UNIT)
    return sizes


def local(context, residual, target, norm_gain, params, momentum, push_weight, mix_num):
    count = lax.axis_size("fsdp")
    replicas = lax.axis_size("rep")
    residual, target, params, momentum = residual[0], target[0], params[0], momentum[0]
    rows, width = params.shape
    features = rows * count

    along_z = [(r, (r - 2) % replicas if r % 2 == 0 else (r + 2) % replicas) for r in range(replicas)]
    along_y = [(r, r ^ 1) for r in range(replicas)]
    over_z = lambda value: lax.ppermute(value, "rep", along_z)
    over_y = lambda value: lax.ppermute(value, "rep", along_y)

    far = with_partner(context[0], count // 2, count)
    near_pieces = gather_low(context[0], count)
    push_row = jnp.broadcast_to(push_weight, (8, 128))
    push_lower = lax.ppermute(push_row, "rep", [(r, (r + 1) % replicas) for r in range(replicas)])
    push_upper = lax.ppermute(push_row, "rep", [(r, (r - 1) % replicas) for r in range(replicas)])
    gain = norm_gain[:, None]
    mix = mix_num.reshape(-1)
    near = near_turned(near_pieces, mix, (gain, push_lower, push_upper, momentum, residual, target))
    far, near = lax.optimization_barrier((far, near))
    pieces = near_pieces + gather_low(far, count)
    total, moment_product, sums, tokens_all, new_push = forward(
        mix,
        push_weight,
        push_lower,
        push_upper,
        params,
        momentum,
        residual,
        target,
        gain,
        near,
        pieces,
    )
    sums = all_sums(sums, count)
    gram = lax.dot_general(tokens_all, tokens_all, NT, preferred_element_type=F32)
    grad, total, sums = second(
        push_weight, total, target, gain, moment_product, gram, sums, features
    )
    sums = all_sums(sums, count)

    arrays = (params, momentum, grad, total, target, gain, tokens_all)
    sizes = chunk_sizes(rows)
    chunks = len(sizes)
    starts = [sum(sizes[:c]) for c in range(chunks)]
    made, crossing, arriving = {}, {}, {}
    held = None
    last = ()
    for c in range(-Z_AHEAD, chunks + Y_AHEAD):
        if 0 <= c < chunks:
            state, master = made[c]
            both = pair_sum(mix, master, state, crossing.pop(c), last)
            arriving[c] = over_y(both)
            last = (both,)
        ahead, behind = c + Z_AHEAD, c - Y_AHEAD
        update = (starts[ahead], arrays, sums) if ahead < chunks else None
        done = None
        if behind >= 0:
            state, master = made.pop(behind)
            done = (starts[behind], rows, master, state, arriving.pop(behind))
        if update and done and sizes[ahead] == sizes[behind]:
            calls = [(sizes[ahead], update, done)]
        else:
            calls = [(sizes[ahead], update, None)] if update else []
            calls += [(sizes[behind], None, done)] if done else []
        for size, update, done in calls:
            out, held = step_call(mix, size, update, done, held, last, features)
            if out:
                made[ahead] = out
                crossing[ahead] = over_z(out[0])
                last = (out[0],)
    return (held[0][None], held[1][None], new_push[0, 0:1])


def solution(mesh):
    return jax.shard_map(
        local,
        mesh=mesh,
        in_specs=(
            P("rep", "fsdp", None),
            P("rep", "fsdp", None),
            P("rep", "fsdp", None),
            P("fsdp"),
            P("rep", "fsdp", None),
            P("rep", "fsdp", None),
            P("rep"),
            P(),
        ),
        out_specs=(P("rep", "fsdp", None), P("rep", "fsdp", None), P("rep")),
        check_vma=False,
    )
```
